512 devices in a mesh: src: 32 (over z, x_lo, core), tgt: 16 (over x_hi, y).
Axes of the slice: x: 4 (x_hi: 2, x_lo: 2; x = x_hi * 2 + x_lo), y: 8, z: 8, core: 2. Of those that a mesh axis runs over, the one named last changes fastest.
Arguments:
- src_codes: bfloat16 [65536, 256], P('src'), may hold values from -127 to 127, as said below
- src_scales: bfloat16 [65536, 2], P('src'), may hold values from 0.0029907227 to 0.029907227
- log_source_mass: float32 [65536], P('src'), may hold values from -4 to 4
- tgt_codes: bfloat16 [32768, 256], P(('tgt', 'src')), may hold values from -127 to 127, as said below
- tgt_scales: bfloat16 [32768, 2], P(('tgt', 'src')), may hold values from 0.0029907227 to 0.029907227
- tgt_potential: bfloat16 [32768], P(('tgt', 'src')), may hold values from -4 to 4
- log_target_mass: float32 [32768], P(('tgt', 'src')), may hold values from -4 to 4
Outputs:
- new_source_potential: float32 [65536], P('src')
- new_target_potential: float32 [32768], P(('tgt', 'src'))
The draws below stay inside these ranges and needn't reach their ends.
Inputs may be any that keep to these rules, and one draw needn't show every extreme that they name: `src_codes`: every entry is a whole number. `tgt_codes`: every entry is a whole number.
All inputs are finite; a program needn't handle non-finite values.
Results may differ from the reference program's by a relative error of at most 0.0004.
Values may be sent and summed in bfloat16 or wider, within the bound.
A program may use at most 64 MiB of HBM per device.

```python
import math
import jax
import jax.numpy as jnp
from jax import lax

D = 256
NBLK = 2
S_DEV = 2048
NS = 65536
NT = 32768
N_SRC = 32


def target_table(key):
    return jax.random.randint(jax.random.fold_in(key, 11), (NT, D), -127, 128)


def draw_tgt_codes(key, part):
    code_table = target_table(key)
    return code_table.astype(jnp.float32).astype(jnp.bfloat16)


def draw_src_codes(key, part):
    code_table = jax.random.randint(jax.random.fold_in(key, 17), (NS, D), -127, 128)
    return code_table.astype(jnp.float32).astype(jnp.bfloat16)


def block_scale(stream_key, shape, cuts, low, top_value):
    gain, own = 1.0, jax.random.fold_in(stream_key, 6)
    for axis_at, parts in cuts:
        steps = jnp.exp(jax.random.uniform(jax.random.fold_in(own, axis_at), (parts,), jnp.float32, low / len(cuts), top_value / len(cuts)))
        gain = gain * jnp.repeat(steps, shape[axis_at] // parts).reshape([-1 if axis == axis_at else 1 for axis in range(len(shape))])
    return gain


def scatter_about(own_key, extent, deviation, limit, split=(), kind=jnp.bfloat16):
    result = jax.random.normal(own_key, extent, jnp.float32) * deviation
    if len(split) > 0:
        result = block_scale(own_key, extent, split, -0.22, 0.18) * result
    return jnp.clip(result, min=-limit, max=limit).astype(kind)


def setup_inputs(seed: int = 0) -> dict:
    key_of = jax.random.split(jax.random.key(seed), 8)
    src_codes = draw_src_codes(jax.random.fold_in(key_of[7], 71), 0)
    src_scales = jnp.clip(jnp.exp(math.log(0.029907227) - 2.3025851 * jax.random.uniform(key_of[1], (NS, NBLK), jnp.float32) ** block_scale(key_of[1], (NS, NBLK), ((0, 32),), -0.2, 0.2)), 0.0029907227, 0.029907227).astype(jnp.bfloat16)
    log_source_mass = scatter_about(key_of[2], (NS,), 1.0, 4.0, ((0, 32),), jnp.float32)
    tgt_codes = draw_tgt_codes(jax.random.fold_in(key_of[7], 71), 0)
    tgt_scales = jnp.clip(jnp.exp(math.log(0.029907227) - 2.3025851 * jax.random.uniform(key_of[4], (NT, NBLK), jnp.float32) ** block_scale(key_of[4], (NT, NBLK), ((0, 512),), -0.2, 0.2)), 0.0029907227, 0.029907227).astype(jnp.bfloat16)
    tgt_potential = scatter_about(key_of[5], (NT,), 1.0, 4.0, ((0, 512),))
    log_target_mass = scatter_about(key_of[6], (NT,), 1.0, 4.0, ((0, 512),), jnp.float32)
    return {"src_codes": src_codes, "src_scales": src_scales, "log_source_mass": log_source_mass, "tgt_codes": tgt_codes, "tgt_scales": tgt_scales, "tgt_potential": tgt_potential, "log_target_mass": log_target_mass}


SMOOTHING_TEMP = 0.25
INVERSE_TEMP = 4.0
FLOOR_VALUE = -1e+30

def block_scores(source_codes, source_scales, target_codes, target_scales):
    feature_count = source_codes.shape[1]
    block_total = source_scales.shape[1]
    block_width = feature_count // block_total
    source_scales = source_scales.astype(jnp.float32)
    target_scales = target_scales.astype(jnp.float32)
    summed = jnp.zeros((source_codes.shape[0], target_codes.shape[0]), jnp.float32)
    for block_index in range(block_total):
        low_edge = block_index * block_width
        product = jnp.dot(source_codes[:, low_edge:low_edge + block_width], target_codes[:, low_edge:low_edge + block_width].T, preferred_element_type=jnp.float32)
        summed = summed + product * (source_scales[:, block_index:block_index + 1] * target_scales[:, block_index][None, :])
    return summed * (1.0 / math.sqrt(feature_count))

def reference(src_codes, src_scales, log_source_mass, tgt_codes, tgt_scales, tgt_potential, log_target_mass):
    code_blocks = src_codes.reshape(N_SRC, S_DEV, D)
    scale_blocks = src_scales.reshape(N_SRC, S_DEV, NBLK)
    target_shift = tgt_potential.astype(jnp.float32)[None, :]

    def row_block(inputs):
        code_rows, scale_rows = inputs
        logits = (target_shift + block_scores(code_rows, scale_rows, tgt_codes, tgt_scales)) * INVERSE_TEMP
        highest = lax.optimization_barrier(jnp.max(logits, axis=1))
        return highest + jnp.log(lax.optimization_barrier(jnp.sum(jnp.exp(logits - highest[:, None]), axis=1)))
    row_logsumexp = lax.map(row_block, (code_blocks, scale_blocks)).reshape(NS)
    refreshed_source = SMOOTHING_TEMP * (log_source_mass - row_logsumexp)
    potential_blocks = refreshed_source.reshape(N_SRC, S_DEV)

    def column_block(running, inputs):
        code_rows, scale_rows, potential_rows = inputs
        logits = (potential_rows[:, None] + block_scores(code_rows, scale_rows, tgt_codes, tgt_scales)) * INVERSE_TEMP
        block_max = lax.optimization_barrier(jnp.max(logits, axis=0))
        block_sum = lax.optimization_barrier(jnp.sum(jnp.exp(logits - block_max[None, :]), axis=0))
        run_max, run_sum = running
        joined = jnp.maximum(run_max, block_max)
        return ((joined, run_sum * jnp.exp(run_max - joined) + block_sum * jnp.exp(block_max - joined)), None)
    starting = (jnp.full((NT,), FLOOR_VALUE, jnp.float32), jnp.zeros((NT,), jnp.float32))
    (col_max, col_sum), unused = lax.scan(column_block, starting, (code_blocks, scale_blocks, potential_blocks))
    column_logsumexp = col_max + jnp.log(col_sum)
    refreshed_target = SMOOTHING_TEMP * (log_target_mass - column_logsumexp)
    return (refreshed_source, refreshed_target)
```

```python
import math

import jax
import jax.numpy as jnp
from jax import lax
from jax.experimental import pallas as pl
from jax.experimental.pallas import tpu as pltpu
from jax.sharding import PartitionSpec as P

F32 = jnp.float32
BF16 = jnp.bfloat16
NT = (((1,), (1,)), ((), ()))
NN = (((1,), (0,)), ((), ()))
MESH = pl.DeviceIdType.MESH

LOG2E = math.log2(math.e)
LN2 = math.log(2.0)
INV_TEMP = 4.0
TEMP = 0.25

SRC = 32
TGT = 16
ROWS = 2048
OWN = 64
ZS = 8


def tree(op, items):
    items = list(items)
    while len(items) > 1:
        items = [
            op(items[i], items[i + 1]) if i + 1 < len(items) else items[i]
            for i in range(0, len(items), 2)
        ]
    return items[0]


def replicate(rows):
    size = rows[0][1]
    lane = lax.broadcasted_iota(jnp.int32, (size, 128), 1)
    down = lax.broadcasted_iota(jnp.int32, (size, 128), 0)
    left = jnp.concatenate(
        [
            jnp.where(lane == down, jnp.broadcast_to(row, (size, 128)), 0.0).astype(BF16)
            for row, _ in rows
        ],
        axis=0,
    )
    return lax.dot_general(left, jnp.ones((128, 128), BF16), NN, preferred_element_type=F32)


def kernel(
    codes_ref,
    sscale_ref,
    smass_ref,
    tcodes_ref,
    tscale_ref,
    tpot_ref,
    tmass_ref,
    u_ref,
    v_ref,
    held,
    aux,
    left,
    right,
    logits,
    peak,
    total,
    scale_row,
    shift_row,
    t_scale,
    t_pot,
    lane_peak,
    lane_sum,
    row_lse,
    col_mine,
    col_lse,
    held_recv,
    aux_recv,
    row_recv,
    col_recv,
    send,
):
    src = lax.axis_index("src")
    tgt = lax.axis_index("tgt")
    z, x, core = src // 4, (src // 2) % 2, src % 2

    def slot(zz, xx, cc):
        return ((zz + 2 * ZS) % ZS) * 4 + xx * 2 + cc

    def codes_copy(piece, to):
        return pltpu.make_async_remote_copy(
            src_ref=held.at[piece],
            dst_ref=held.at[piece],
            send_sem=send.at[0],
            recv_sem=held_recv.at[piece],
            device_id={"src": to},
            device_id_type=MESH,
        )

    def aux_copy(piece, to):
        return pltpu.make_async_remote_copy(
            src_ref=aux.at[piece],
            dst_ref=aux.at[piece],
            send_sem=send.at[1],
            recv_sem=aux_recv.at[piece],
            device_id={"src": to},
            device_id_type=MESH,
        )

    def push(piece, to):
        codes_copy(piece, to).start()
        aux_copy(piece, to).start()

    def arrived(piece):
        codes_copy(piece, src).wait_recv()
        aux_copy(piece, src).wait_recv()

    up, down = slot(z + 1, x, core), slot(z - 1, x, core)
    partner, sibling = slot(z, 1 - x, core), slot(z, x, 1 - core)

    barrier = pltpu.get_barrier_semaphore()

    def greet_src(k, _):
        pl.semaphore_signal(
            barrier, inc=1, device_id={"src": (src + k) % SRC}, device_id_type=MESH
        )
        return 0

    def greet_tgt(k, _):
        pl.semaphore_signal(
            barrier, inc=1, device_id={"tgt": (tgt + k) % TGT}, device_id_type=MESH
        )
        return 0

    lax.fori_loop(1, SRC, greet_src, 0)
    lax.fori_loop(1, TGT, greet_tgt, 0)

    held[src] = tcodes_ref[...]
    own_scale = tscale_ref[...].astype(F32)
    own_pot = tpot_ref[...].astype(F32)
    blank = jnp.zeros((1, OWN), F32)
    aux[src] = jnp.concatenate(
        [own_scale[0:1], blank, own_scale[1:2], blank, own_pot, blank], axis=1
    )

    pl.semaphore_wait(barrier, SRC + TGT - 2)

    push(src, up)
    push(src, down)
    push(src, partner)
    push(src, sibling)

    source_scale = sscale_ref[...].astype(F32)

    def source_part(first, last):
        rows = [
            (source_scale[b : b + 1, k * 128 : k * 128 + 128], 128)
            for b in range(2)
            for k in range(first, last)
        ]
        wide = replicate(rows)
        many = (last - first) * 128
        ratio = wide[many:] / wide[:many]
        at = slice(first * 128, last * 128)
        scaled = codes_ref[at, 128:256].astype(F32) * ratio
        high = scaled.astype(BF16)
        left[at, 0:128] = codes_ref[at, 0:128]
        left[at, 128:256] = high
        left[at, 256:384] = high
        left[at, 384:512] = (scaled - high.astype(F32)).astype(BF16)

    source_part(0, 8)

    arrived(partner)
    push(partner, up)
    push(partner, down)
    push(partner, sibling)
    for side, onward in ((-1, up), (1, down)):
        piece = slot(z + side, x, core)
        arrived(piece)
        push(piece, onward)
        push(piece, sibling)

    source_part(8, 16)
    scale_row[...] = jnp.broadcast_to(source_scale[0:1] * (INV_TEMP * LOG2E / 16.0), (8, ROWS))
    peak[...] = jnp.full((8, ROWS), -1e30, F32)
    total[...] = jnp.zeros((8, ROWS), F32)

    for side, onward in ((-1, up), (1, down)):
        piece = slot(z + side, 1 - x, core)
        arrived(piece)
        push(piece, onward)
        push(piece, sibling)

    def chunk(k, _):
        far = (k + 1) // 2 + 1
        own_column = k % 2 == 1

        @pl.when(jnp.logical_and(k >= 1, k <= 2))
        def _():
            xx = jnp.where(own_column, x, 1 - x)
            for side, onward in ((-1, up), (1, down)):
                piece = slot(z + side * 2, xx, core)
                arrived(piece)
                push(piece, onward)
                push(piece, sibling)

        @pl.when(jnp.logical_and(k >= 3, k <= 4))
        def _():
            xx = jnp.where(own_column, x, 1 - x)
            for side, onward in ((-1, up), (1, down)):
                piece = slot(z + side * 3, xx, core)
                arrived(piece)

                @pl.when(own_column if side == -1 else jnp.logical_not(own_column))
                def _():
                    push(piece, onward)

                push(piece, sibling)

        @pl.when(k == 5)
        def _():
            for xx in (x, 1 - x):
                piece = slot(z + 4, xx, core)
                arrived(piece)
                push(piece, sibling)

        away = (k + 1) // 2
        zz = (z + jnp.where(k % 2 == 1, away, -away) + 2 * ZS) % ZS
        for xx in (0, 1):
            arrived(slot(zz, xx, 1 - core))

        first = pl.multiple_of(zz * 256, 256)
        side_rows = [aux[zz * 4 + p] for p in range(4)]
        wide = replicate(
            [(row[:, b * 128 : b * 128 + 128], OWN) for b in range(3) for row in side_rows]
        )
        t_scale[...] = wide[0:256]
        t_pot[...] = wide[512:768] * (INV_TEMP * LOG2E)
        pieces = held[pl.ds(zz * 4, 4)].reshape(256, 256)
        scaled = pieces[:, 128:256].astype(F32) * (wide[256:512] / wide[0:256])
        high = scaled.astype(BF16)
        right[:, 0:128] = pieces[:, 0:128]
        right[:, 128:256] = high
        right[:, 256:384] = (scaled - high.astype(F32)).astype(BF16)
        right[:, 384:512] = high

        for n in range(8):
            product = lax.dot_general(
                right[...], left[n * 256 : n * 256 + 256, :], NT, preferred_element_type=F32
            )
            tiles = [slice((2 * n + i) * 128, (2 * n + i) * 128 + 128) for i in range(2)]
            s_scale = [scale_row[:, t] for t in tiles]
            high_mark = [peak[:, t] for t in tiles]
            summed = [total[:, t] for t in tiles]
            for g0 in range(0, 32, 4):
                values = [[], []]
                for g in range(g0, g0 + 4):
                    down8 = slice(g * 8, g * 8 + 8)
                    scale, pot = t_scale[down8, :], t_pot[down8, :]
                    for i, t in enumerate(tiles):
                        value = product[down8, i * 128 : i * 128 + 128] * s_scale[i] * scale + pot
                        logits[pl.ds(first + g * 8, 8), t] = value
                        values[i].append(value)
                for i in range(2):
                    mark = jnp.maximum(high_mark[i], tree(jnp.maximum, values[i]))
                    added = tree(jnp.add, [jnp.exp2(value - mark) for value in values[i]])
                    summed[i] = summed[i] * jnp.exp2(high_mark[i] - mark) + added
                    high_mark[i] = mark
            for i, t in enumerate(tiles):
                peak[:, t] = high_mark[i]
                total[:, t] = summed[i]
        return 0

    lax.fori_loop(0, ZS, chunk, 0)

    for k in range(16):
        t = slice(k * 128, k * 128 + 128)
        mark = jnp.max(peak[:, t], axis=0, keepdims=True)
        row_sum = jnp.sum(total[:, t] * jnp.exp2(peak[:, t] - mark), axis=0, keepdims=True)
        row_lse[tgt, k : k + 1, :] = mark + jnp.log2(row_sum)

    def row_copy(group, to):
        return pltpu.make_async_remote_copy(
            src_ref=row_lse.at[group],
            dst_ref=row_lse.at[group],
            send_sem=send.at[2],
            recv_sem=row_recv.at[group],
            device_id={"tgt": to},
            device_id_type=MESH,
        )

    def row_push(k, _):
        row_copy(tgt, (tgt + k) % TGT).start()
        return 0

    def row_wait(k, _):
        row_copy((tgt + k) % TGT, tgt).wait_recv()
        return 0

    lax.fori_loop(1, TGT, row_push, 0)
    lax.fori_loop(1, TGT, row_wait, 0)

    every = [row_lse[g] for g in range(TGT)]
    mark = tree(jnp.maximum, every)
    joined = mark + jnp.log2(tree(jnp.add, [jnp.exp2(one - mark) for one in every]))
    mass = smass_ref[...]
    u_ref[...] = TEMP * (mass - LN2 * joined)
    shift = LOG2E * mass - joined
    for k in range(16):
        shift_row[:, k * 128 : k * 128 + 128] = jnp.broadcast_to(shift[k : k + 1, :], (8, 128))

    def col_copy(to):
        return pltpu.make_async_remote_copy(
            src_ref=col_mine.at[pl.ds(to // 2, 1)],
            dst_ref=col_lse.at[pl.ds(src, 1)],
            send_sem=send.at[3],
            recv_sem=col_recv.at[src],
            device_id={"src": to},
            device_id_type=MESH,
        )

    def half(h, _):
        def lanes(b, _):
            for g in range(64):
                down8 = pl.ds(pl.multiple_of(h * 1024 + b * 512 + g * 8, 8), 8)
                values = [
                    logits[down8, k * 128 : k * 128 + 128] + shift_row[:, k * 128 : k * 128 + 128]
                    for k in range(16)
                ]
                mark = tree(jnp.maximum, values)
                at = pl.ds(pl.multiple_of(b * 512 + g * 8, 8), 8)
                lane_peak[at, :] = mark
                lane_sum[at, :] = tree(jnp.add, [jnp.exp2(value - mark) for value in values])
            return 0

        lax.fori_loop(0, 2, lanes, 0)
        for q in range(8):
            at = slice(q * 128, q * 128 + 128)
            peaks, sums = lane_peak[at, :].T, lane_sum[at, :].T
            mark = jnp.max(peaks, axis=0, keepdims=True)
            col_mine[pl.ds(h * 8 + q, 1), :] = mark + jnp.log2(
                jnp.sum(sums * jnp.exp2(peaks - mark), axis=0, keepdims=True)
            )

        def col_push(k, _):
            to = h * 16 + k

            @pl.when(to != src)
            def _():
                col_copy(to).start()

            return 0

        lax.fori_loop(0, 16, col_push, 0)
        return 0

    lax.fori_loop(0, 2, half, 0)
    col_lse[pl.ds(src, 1), :] = col_mine[pl.ds(src // 2, 1), :]

    def col_wait(k, _):
        other = (src + k) % SRC
        pltpu.make_async_remote_copy(
            src_ref=col_mine.at[pl.ds(0, 1)],
            dst_ref=col_lse.at[pl.ds(other, 1)],
            send_sem=send.at[3],
            recv_sem=col_recv.at[other],
            device_id={"src": src},
            device_id_type=MESH,
        ).wait_recv()
        return 0

    lax.fori_loop(1, SRC, col_wait, 0)
    partial = col_lse[...]
    mark = jnp.max(partial, axis=0, keepdims=True)
    joined = mark + jnp.log2(jnp.sum(jnp.exp2(partial - mark), axis=0, keepdims=True))
    mine = jnp.where(core == 1, joined[:, 64:128], joined[:, 0:64])
    v_ref[...] = TEMP * (tmass_ref[...] - (LN2 * mine - INV_TEMP * own_pot))

    for k, (buffer, many) in enumerate(
        ((held, SRC - 1), (aux, SRC - 1), (row_lse, TGT - 1), (col_lse, SRC - 1))
    ):
        part = buffer.at[pl.ds(0, many)]
        pltpu.make_async_copy(part, part, send.at[k]).wait()


def per_device(src_codes, src_scales, log_source_mass, tgt_codes, tgt_scales, tgt_potential, log_target_mass):
    vmem = pl.BlockSpec(memory_space=pltpu.VMEM)
    u, v = pl.pallas_call(
        kernel,
        out_shape=(
            jax.ShapeDtypeStruct((16, 128), F32),
            jax.ShapeDtypeStruct((1, OWN), F32),
        ),
        in_specs=[vmem] * 7,
        out_specs=(vmem, vmem),
        scratch_shapes=[
            pltpu.VMEM((SRC, OWN, 256), BF16),
            pltpu.VMEM((SRC, 1, 384), F32),
            pltpu.VMEM((ROWS, 512), BF16),
            pltpu.VMEM((256, 512), BF16),
            pltpu.VMEM((ROWS, ROWS), F32),
            pltpu.VMEM((8, ROWS), F32),
            pltpu.VMEM((8, ROWS), F32),
            pltpu.VMEM((8, ROWS), F32),
            pltpu.VMEM((8, ROWS), F32),
            pltpu.VMEM((256, 128), F32),
            pltpu.VMEM((256, 128), F32),
            pltpu.VMEM((1024, 128), F32),
            pltpu.VMEM((1024, 128), F32),
            pltpu.VMEM((TGT, 16, 128), F32),
            pltpu.VMEM((16, 128), F32),
            pltpu.VMEM((SRC, 128), F32),
            pltpu.SemaphoreType.DMA((SRC,)),
            pltpu.SemaphoreType.DMA((SRC,)),
            pltpu.SemaphoreType.DMA((TGT,)),
            pltpu.SemaphoreType.DMA((SRC,)),
            pltpu.SemaphoreType.DMA((4,)),
        ],
        compiler_params=pltpu.CompilerParams(
            collective_id=0, has_side_effects=True, vmem_limit_bytes=44 << 20
        ),
        cost_estimate=pl.CostEstimate(
            flops=2 * ROWS * ROWS * 512, bytes_accessed=2 << 20, transcendentals=2 * ROWS * ROWS
        ),
    )(
        src_codes,
        src_scales.T,
        log_source_mass.reshape(16, 128),
        tgt_codes,
        tgt_scales.T,
        tgt_potential.reshape(1, OWN),
        log_target_mass.reshape(1, OWN),
    )
    return u.reshape(ROWS), v.reshape(OWN)


def solution(mesh):
    return jax.shard_map(
        per_device,
        mesh=mesh,
        in_specs=(
            P("src", None),
            P("src", None),
            P("src"),
            P(("tgt", "src"), None),
            P(("tgt", "src"), None),
            P(("tgt", "src")),
            P(("tgt", "src")),
        ),
        out_specs=(P("src"), P(("tgt", "src"))),
        check_vma=False,
    )
```

```python
import math

import jax
import jax.numpy as jnp
from jax import lax
from jax.experimental import pallas as pl
from jax.experimental.pallas import tpu as pltpu
from jax.sharding import PartitionSpec as P

F32 = jnp.float32
BF16 = jnp.bfloat16
NT = (((1,), (1,)), ((), ()))
NN = (((1,), (0,)), ((), ()))
MESH = pl.DeviceIdType.MESH

LOG2E = math.log2(math.e)
LN2 = math.log(2.0)
INV_TEMP = 4.0
TEMP = 0.25

SRC = 32
TGT = 16
ROWS = 2048
OWN = 64
ZS = 8


def tree(op, items):
    items = list(items)
    while len(items) > 1:
        items = [
            op(items[i], items[i + 1]) if i + 1 < len(items) else items[i]
            for i in range(0, len(items), 2)
        ]
    return items[0]


def replicate(rows):
    size = rows[0][1]
    lane = lax.broadcasted_iota(jnp.int32, (size, 128), 1)
    down = lax.broadcasted_iota(jnp.int32, (size, 128), 0)
    left = jnp.concatenate(
        [
            jnp.where(lane == down, jnp.broadcast_to(row, (size, 128)), 0.0).astype(BF16)
            for row, _ in rows
        ],
        axis=0,
    )
    return lax.dot_general(left, jnp.ones((128, 128), BF16), NN, preferred_element_type=F32)


def kernel(
    codes_hbm,
    sscale_hbm,
    smass_hbm,
    tcodes_hbm,
    tscale_hbm,
    tpot_hbm,
    tmass_hbm,
    u_ref,
    v_ref,
    codes_ref,
    sscale_ref,
    smass_ref,
    tscale_ref,
    tpot_ref,
    tmass_ref,
    held,
    aux,
    left,
    right,
    logits,
    peak,
    total,
    scale_row,
    shift_row,
    t_scale,
    t_pot,
    lane_peak,
    lane_sum,
    row_lse,
    col_mine,
    col_lse,
    held_recv,
    aux_recv,
    row_recv,
    col_recv,
    send,
    local,
):
    src = lax.axis_index("src")
    tgt = lax.axis_index("tgt")
    z, x, core = src // 4, (src // 2) & 1, src & 1

    def slot(zz, xx, cc):
        return (zz & (ZS - 1)) * 4 + xx * 2 + cc

    def codes_copy(piece, to):
        return pltpu.make_async_remote_copy(
            src_ref=held.at[piece],
            dst_ref=held.at[piece],
            send_sem=send.at[0],
            recv_sem=held_recv.at[piece],
            device_id={"src": to},
            device_id_type=MESH,
        )

    def aux_copy(piece, to):
        return pltpu.make_async_remote_copy(
            src_ref=aux.at[piece],
            dst_ref=aux.at[piece],
            send_sem=send.at[1],
            recv_sem=aux_recv.at[piece],
            device_id={"src": to},
            device_id_type=MESH,
        )

    def push(piece, to):
        codes_copy(piece, to).start()
        aux_copy(piece, to).start()

    def arrived(piece):
        codes_copy(piece, src).wait_recv()
        aux_copy(piece, src).wait_recv()

    partner, sibling = slot(z, 1 - x, core), slot(z, x, 1 - core)

    barrier = pltpu.get_barrier_semaphore()

    def greet_src(k, _):
        pl.semaphore_signal(
            barrier, inc=1, device_id={"src": (src + k) & (SRC - 1)}, device_id_type=MESH
        )
        return 0

    def greet_tgt(k, _):
        pl.semaphore_signal(
            barrier, inc=1, device_id={"tgt": (tgt + k) & (TGT - 1)}, device_id_type=MESH
        )
        return 0

    lax.fori_loop(1, SRC, greet_src, 0)
    lax.fori_loop(1, TGT, greet_tgt, 0)

    fetches = [
        pltpu.make_async_copy(a, b, local.at[k])
        for k, (a, b) in enumerate(
            (
                (tcodes_hbm, held.at[src]),
                (tscale_hbm, tscale_ref),
                (tpot_hbm, tpot_ref),
                (sscale_hbm, sscale_ref),
                (codes_hbm, codes_ref),
                (smass_hbm, smass_ref),
                (tmass_hbm, tmass_ref),
            )
        )
    ]
    for fetch in fetches:
        fetch.start()
    for fetch in fetches[:3]:
        fetch.wait()
    own_scale = tscale_ref[...].astype(F32)
    own_pot = tpot_ref[...].astype(F32)
    blank = jnp.zeros((1, OWN), F32)
    aux[src] = jnp.concatenate(
        [own_scale[0:1], blank, own_scale[1:2], blank, own_pot, blank], axis=1
    )

    pl.semaphore_wait(barrier, SRC + TGT - 2)

    push(src, sibling)
    push(src, slot(z + 1, x, core))
    push(src, slot(z - 1, x, core))
    push(src, partner)
    for away in (2, -2, 3, -3, 4):
        push(src, slot(z + away, x, core))
    for fetch in fetches[3:]:
        fetch.wait()

    source_scale = sscale_ref[...].astype(F32)

    def source_part(first, last):
        rows = [
            (source_scale[b : b + 1, k * 128 : k * 128 + 128], 128)
            for b in range(2)
            for k in range(first, last)
        ]
        wide = replicate(rows)
        many = (last - first) * 128
        ratio = wide[many:] / wide[:many]
        at = slice(first * 128, last * 128)
        scaled = codes_ref[at, 128:256].astype(F32) * ratio
        high = scaled.astype(BF16)
        left[at, 0:128] = codes_ref[at, 0:128]
        left[at, 128:256] = high
        left[at, 256:384] = high
        left[at, 384:512] = (scaled - high.astype(F32)).astype(BF16)

    def own_column(*steps):
        for step in steps:
            piece = slot(z + step, x, core)
            arrived(piece)
            push(piece, partner)
            push(piece, sibling)

    def other_column(*steps):
        for step in steps:
            piece = slot(z + step, 1 - x, core)
            arrived(piece)
            push(piece, sibling)

    source_part(0, 8)
    other_column(0)
    own_column(1, -1)
    source_part(8, 16)
    scale_row[...] = jnp.broadcast_to(source_scale[0:1] * (INV_TEMP * LOG2E / 16.0), (8, ROWS))
    peak[...] = jnp.full((8, ROWS), -1e30, F32)
    total[...] = jnp.zeros((8, ROWS), F32)
    own_column(2, -2)

    def chunk(k, _):
        @pl.when(k == 1)
        def _():
            own_column(3, -3)

        @pl.when(k == 2)
        def _():
            own_column(4)

        @pl.when(jnp.logical_and(k >= 2, k <= 4))
        def _():
            other_column(k - 1, 1 - k)

        @pl.when(k == 5)
        def _():
            other_column(4)

        away = jnp.where(k >= 4, k - 3, k)
        beside = jnp.logical_or(k == 0, k == 7)
        x_a = jnp.where(jnp.logical_and(k >= 4, k <= 6), 1 - x, x)
        x_b = jnp.where(beside, 1 - x, x_a)
        z_b = jnp.where(beside, z + away, z - away)
        chips = (slot(z + away, x_a, 0), slot(z_b, x_b, 0))
        for chip in chips:
            arrived(chip + 1 - core)

        side_rows = [aux[chip + c] for chip in chips for c in (0, 1)]
        wide = replicate(
            [(row[:, b * 128 : b * 128 + 128], OWN) for b in range(3) for row in side_rows]
        )
        t_scale[...] = wide[0:256]
        t_pot[...] = wide[512:768] * (INV_TEMP * LOG2E)
        pieces = jnp.concatenate([held[pl.ds(chip, 2)].reshape(128, 256) for chip in chips])
        scaled = pieces[:, 128:256].astype(F32) * (wide[256:512] / wide[0:256])
        high = scaled.astype(BF16)
        right[:, 0:128] = pieces[:, 0:128]
        right[:, 128:256] = high
        right[:, 256:384] = (scaled - high.astype(F32)).astype(BF16)
        right[:, 384:512] = high

        for n in range(8):
            product = lax.dot_general(
                right[...], left[n * 256 : n * 256 + 256, :], NT, preferred_element_type=F32
            )
            tiles = [slice((2 * n + i) * 128, (2 * n + i) * 128 + 128) for i in range(2)]
            s_scale = [scale_row[:, t] for t in tiles]
            high_mark = [peak[:, t] for t in tiles]
            summed = [total[:, t] for t in tiles]
            for g0 in range(0, 32, 4):
                values = [[], []]
                for g in range(g0, g0 + 4):
                    down8 = slice(g * 8, g * 8 + 8)
                    scale, pot = t_scale[down8, :], t_pot[down8, :]
                    for i, t in enumerate(tiles):
                        value = product[down8, i * 128 : i * 128 + 128] * s_scale[i] * scale + pot
                        at = pl.multiple_of(chips[g // 16] * OWN + (g % 16) * 8, 8)
                        logits[pl.ds(at, 8), t] = value
                        values[i].append(value)
                for i in range(2):
                    mark = jnp.maximum(high_mark[i], tree(jnp.maximum, values[i]))
                    added = tree(jnp.add, [jnp.exp2(value - mark) for value in values[i]])
                    summed[i] = summed[i] * jnp.exp2(high_mark[i] - mark) + added
                    high_mark[i] = mark
            for i, t in enumerate(tiles):
                peak[:, t] = high_mark[i]
                total[:, t] = summed[i]
        return 0

    lax.fori_loop(0, ZS, chunk, 0)

    for k in range(16):
        t = slice(k * 128, k * 128 + 128)
        mark = jnp.max(peak[:, t], axis=0, keepdims=True)
        row_sum = jnp.sum(total[:, t] * jnp.exp2(peak[:, t] - mark), axis=0, keepdims=True)
        row_lse[tgt, k : k + 1, :] = mark + jnp.log2(row_sum)

    def row_copy(group, to):
        return pltpu.make_async_remote_copy(
            src_ref=row_lse.at[group],
            dst_ref=row_lse.at[group],
            send_sem=send.at[2],
            recv_sem=row_recv.at[group],
            device_id={"tgt": to},
            device_id_type=MESH,
        )

    others = [(a, b) for a in (0, 1) for b in range(ZS) if a or b]
    for a, b in sorted(others, key=lambda ab: -2 * ab[0] - min(ab[1], ZS - ab[1])):
        row_copy(tgt, ((tgt // ZS) ^ a) * ZS + ((tgt + b) & (ZS - 1))).start()

    def row_wait(k, _):
        row_copy((tgt + k) & (TGT - 1), tgt).wait_recv()
        return 0

    lax.fori_loop(1, TGT, row_wait, 0)

    every = [row_lse[g] for g in range(TGT)]
    mark = tree(jnp.maximum, every)
    joined = mark + jnp.log2(tree(jnp.add, [jnp.exp2(one - mark) for one in every]))
    mass = smass_ref[...]
    u_ref[...] = TEMP * (mass - LN2 * joined)
    shift = LOG2E * mass - joined
    for k in range(16):
        shift_row[:, k * 128 : k * 128 + 128] = jnp.broadcast_to(shift[k : k + 1, :], (8, 128))

    def col_copy(to):
        return pltpu.make_async_remote_copy(
            src_ref=col_mine.at[pl.ds(to // 2, 1)],
            dst_ref=col_lse.at[pl.ds(src, 1)],
            send_sem=send.at[3],
            recv_sem=col_recv.at[src],
            device_id={"src": to},
            device_id_type=MESH,
        )

    def half(h, _):
        def place(n):
            return (z + 2 + h * 4 + n) & (ZS - 1)

        def lanes(b, _):
            for g in range(32):
                down8 = pl.ds(pl.multiple_of(place(b) * 256 + g * 8, 8), 8)
                values = [
                    logits[down8, k * 128 : k * 128 + 128] + shift_row[:, k * 128 : k * 128 + 128]
                    for k in range(16)
                ]
                mark = tree(jnp.maximum, values)
                at = pl.ds(pl.multiple_of(b * 256 + g * 8, 8), 8)
                lane_peak[at, :] = mark
                lane_sum[at, :] = tree(jnp.add, [jnp.exp2(value - mark) for value in values])
            return 0

        lax.fori_loop(0, 4, lanes, 0)
        for q in range(8):
            at = slice(q * 128, q * 128 + 128)
            peaks, sums = lane_peak[at, :].T, lane_sum[at, :].T
            mark = jnp.max(peaks, axis=0, keepdims=True)
            col_mine[pl.ds(place(q // 2) * 2 + q % 2, 1), :] = mark + jnp.log2(
                jnp.sum(sums * jnp.exp2(peaks - mark), axis=0, keepdims=True)
            )

        def col_push(k, _):
            to = place(k // 4) * 4 + ((src + k) & 3)

            @pl.when(to != src)
            def _():
                col_copy(to).start()

            return 0

        lax.fori_loop(0, 16, col_push, 0)
        return 0

    lax.fori_loop(0, 2, half, 0)
    col_lse[pl.ds(src, 1), :] = col_mine[pl.ds(src // 2, 1), :]

    def col_wait(k, _):
        other = (src + k) & (SRC - 1)
        pltpu.make_async_remote_copy(
            src_ref=col_mine.at[pl.ds(0, 1)],
            dst_ref=col_lse.at[pl.ds(other, 1)],
            send_sem=send.at[3],
            recv_sem=col_recv.at[other],
            device_id={"src": src},
            device_id_type=MESH,
        ).wait_recv()
        return 0

    lax.fori_loop(1, SRC, col_wait, 0)
    partial = col_lse[...]
    mark = jnp.max(partial, axis=0, keepdims=True)
    joined = mark + jnp.log2(jnp.sum(jnp.exp2(partial - mark), axis=0, keepdims=True))
    mine = jnp.where(core == 1, joined[:, 64:128], joined[:, 0:64])
    v_ref[...] = TEMP * (tmass_ref[...] - (LN2 * mine - INV_TEMP * own_pot))

    for k, (buffer, many) in enumerate(
        ((held, SRC - 1), (aux, SRC - 1), (row_lse, TGT - 1), (col_lse, SRC - 1))
    ):
        part = buffer.at[pl.ds(0, many)]
        pltpu.make_async_copy(part, part, send.at[k]).wait()


def per_device(src_codes, src_scales, log_source_mass, tgt_codes, tgt_scales, tgt_potential, log_target_mass):
    vmem = pl.BlockSpec(memory_space=pltpu.VMEM)
    u, v = pl.pallas_call(
        kernel,
        out_shape=(
            jax.ShapeDtypeStruct((16, 128), F32),
            jax.ShapeDtypeStruct((1, OWN), F32),
        ),
        in_specs=[pl.BlockSpec(memory_space=pltpu.HBM)] * 7,
        out_specs=(vmem, vmem),
        scratch_shapes=[
            pltpu.VMEM((ROWS, 256), BF16),
            pltpu.VMEM((2, ROWS), BF16),
            pltpu.VMEM((16, 128), F32),
            pltpu.VMEM((2, OWN), BF16),
            pltpu.VMEM((1, OWN), BF16),
            pltpu.VMEM((1, OWN), F32),
            pltpu.VMEM((SRC, OWN, 256), BF16),
            pltpu.VMEM((SRC, 1, 384), F32),
            pltpu.VMEM((ROWS, 512), BF16),
            pltpu.VMEM((256, 512), BF16),
            pltpu.VMEM((ROWS, ROWS), F32),
            pltpu.VMEM((8, ROWS), F32),
            pltpu.VMEM((8, ROWS), F32),
            pltpu.VMEM((8, ROWS), F32),
            pltpu.VMEM((8, ROWS), F32),
            pltpu.VMEM((256, 128), F32),
            pltpu.VMEM((256, 128), F32),
            pltpu.VMEM((1024, 128), F32),
            pltpu.VMEM((1024, 128), F32),
            pltpu.VMEM((TGT, 16, 128), F32),
            pltpu.VMEM((16, 128), F32),
            pltpu.VMEM((SRC, 128), F32),
            pltpu.SemaphoreType.DMA((SRC,)),
            pltpu.SemaphoreType.DMA((SRC,)),
            pltpu.SemaphoreType.DMA((TGT,)),
            pltpu.SemaphoreType.DMA((SRC,)),
            pltpu.SemaphoreType.DMA((4,)),
            pltpu.SemaphoreType.DMA((7,)),
        ],
        compiler_params=pltpu.CompilerParams(
            collective_id=0, has_side_effects=True, vmem_limit_bytes=62 << 20
        ),
        cost_estimate=pl.CostEstimate(
            flops=2 * ROWS * ROWS * 512, bytes_accessed=2 << 20, transcendentals=2 * ROWS * ROWS
        ),
    )(
        src_codes,
        src_scales.T,
        log_source_mass.reshape(16, 128),
        tgt_codes,
        tgt_scales.T,
        tgt_potential.reshape(1, OWN),
        log_target_mass.reshape(1, OWN),
    )
    return u.reshape(ROWS), v.reshape(OWN)


def solution(mesh):
    return jax.shard_map(
        per_device,
        mesh=mesh,
        in_specs=(
            P("src", None),
            P("src", None),
            P("src"),
            P(("tgt", "src"), None),
            P(("tgt", "src"), None),
            P(("tgt", "src")),
            P(("tgt", "src")),
        ),
        out_specs=(P("src"), P(("tgt", "src"))),
        check_vma=False,
    )
```

```python
import math

import jax
import jax.numpy as jnp
from jax import lax
from jax.experimental import pallas as pl
from jax.experimental.pallas import tpu as pltpu
from jax.sharding import PartitionSpec as P

F32 = jnp.float32
BF16 = jnp.bfloat16
NT = (((1,), (1,)), ((), ()))
NN = (((1,), (0,)), ((), ()))
MESH = pl.DeviceIdType.MESH

LOG2E = math.log2(math.e)
LN2 = math.log(2.0)
INV_TEMP = 4.0
TEMP = 0.25

SRC = 32
TGT = 16
ROWS = 2048
OWN = 64
ZS = 8


def tree(op, items):
    items = list(items)
    while len(items) > 1:
        items = [
            op(items[i], items[i + 1]) if i + 1 < len(items) else items[i]
            for i in range(0, len(items), 2)
        ]
    return items[0]


def replicate(rows):
    size = rows[0][1]
    lane = lax.broadcasted_iota(jnp.int32, (size, 128), 1)
    down = lax.broadcasted_iota(jnp.int32, (size, 128), 0)
    left = jnp.concatenate(
        [
            jnp.where(lane == down, jnp.broadcast_to(row, (size, 128)), 0.0).astype(BF16)
            for row, _ in rows
        ],
        axis=0,
    )
    return lax.dot_general(left, jnp.ones((128, 128), BF16), NN, preferred_element_type=F32)


def kernel(
    codes_hbm,
    sscale_hbm,
    smass_hbm,
    tcodes_hbm,
    tscale_hbm,
    tpot_hbm,
    tmass_hbm,
    u_ref,
    v_ref,
    codes_ref,
    sscale_ref,
    smass_ref,
    tscale_ref,
    tpot_ref,
    tmass_ref,
    held,
    aux,
    left,
    right,
    logits,
    peak,
    total,
    scale_row,
    shift_row,
    t_scale,
    t_pot,
    lane_peak,
    lane_sum,
    row_lse,
    col_mine,
    col_lse,
    held_recv,
    aux_recv,
    row_recv,
    col_recv,
    send,
    local,
):
    src = lax.axis_index("src")
    tgt = lax.axis_index("tgt")
    z, x, core = src // 4, (src // 2) & 1, src & 1

    def slot(zz, xx, cc):
        return (zz & (ZS - 1)) * 4 + xx * 2 + cc

    def codes_copy(piece, to):
        return pltpu.make_async_remote_copy(
            src_ref=held.at[piece],
            dst_ref=held.at[piece],
            send_sem=send.at[0],
            recv_sem=held_recv.at[piece],
            device_id={"src": to},
            device_id_type=MESH,
        )

    def aux_copy(piece, to):
        return pltpu.make_async_remote_copy(
            src_ref=aux.at[piece],
            dst_ref=aux.at[piece],
            send_sem=send.at[1],
            recv_sem=aux_recv.at[piece],
            device_id={"src": to},
            device_id_type=MESH,
        )

    def push(piece, to):
        codes_copy(piece, to).start()
        aux_copy(piece, to).start()

    def arrived(piece):
        codes_copy(piece, src).wait_recv()
        aux_copy(piece, src).wait_recv()

    partner, sibling = slot(z, 1 - x, core), slot(z, x, 1 - core)

    barrier = pltpu.get_barrier_semaphore()

    def greet(other):
        pl.semaphore_signal(barrier, inc=1, device_id={"src": other}, device_id_type=MESH)

    def greet_tgt(k, _):
        pl.semaphore_signal(
            barrier, inc=1, device_id={"tgt": (tgt + k) & (TGT - 1)}, device_id_type=MESH
        )
        return 0

    near = [slot(z + away, x, core) for away in (4, 3, -3, 2, -2, 1, -1)] + [partner, sibling]
    lax.fori_loop(1, TGT, greet_tgt, 0)
    for other in near:
        greet(other)

    fetches = [
        pltpu.make_async_copy(a, b, local.at[k])
        for k, (a, b) in enumerate(
            (
                (tcodes_hbm, held.at[src]),
                (tscale_hbm, tscale_ref),
                (tpot_hbm, tpot_ref),
                (sscale_hbm, sscale_ref),
                (codes_hbm, codes_ref),
                (smass_hbm, smass_ref),
                (tmass_hbm, tmass_ref),
            )
        )
    ]
    for fetch in fetches:
        fetch.start()
    for fetch in fetches[:3]:
        fetch.wait()
    own_scale = tscale_ref[...].astype(F32)
    own_pot = tpot_ref[...].astype(F32)
    blank = jnp.zeros((1, OWN), F32)
    aux[src] = jnp.concatenate(
        [own_scale[0:1], blank, own_scale[1:2], blank, own_pot, blank], axis=1
    )

    pl.semaphore_wait(barrier, len(near) + TGT - 1)

    push(src, sibling)
    push(src, slot(z + 1, x, core))
    push(src, slot(z - 1, x, core))
    push(src, partner)
    for away in (2, -2, 3, -3, 4):
        push(src, slot(z + away, x, core))
    for fetch in fetches[3:]:
        fetch.wait()

    source_scale = sscale_ref[...].astype(F32)

    def source_part(first, last):
        rows = [
            (source_scale[b : b + 1, k * 128 : k * 128 + 128], 128)
            for b in range(2)
            for k in range(first, last)
        ]
        wide = replicate(rows)
        many = (last - first) * 128
        ratio = wide[many:] / wide[:many]
        at = slice(first * 128, last * 128)
        scaled = codes_ref[at, 128:256].astype(F32) * ratio
        high = scaled.astype(BF16)
        left[at, 0:128] = codes_ref[at, 0:128]
        left[at, 128:256] = high
        left[at, 256:384] = high
        left[at, 384:512] = (scaled - high.astype(F32)).astype(BF16)

    def own_column(*steps):
        for step in steps:
            piece = slot(z + step, x, core)
            arrived(piece)
            push(piece, partner)
            push(piece, sibling)

    def other_column(*steps):
        for step in steps:
            piece = slot(z + step, 1 - x, core)
            arrived(piece)
            push(piece, sibling)

    source_part(0, 8)
    other_column(0)
    own_column(1, -1)
    source_part(8, 16)
    scale_row[...] = jnp.broadcast_to(source_scale[0:1] * (INV_TEMP * LOG2E / 16.0), (8, ROWS))
    peak[...] = jnp.full((8, ROWS), -1e30, F32)
    total[...] = jnp.zeros((8, ROWS), F32)
    own_column(2, -2)

    def chunk(k, _):
        @pl.when(k == 1)
        def _():
            own_column(3, -3)

        @pl.when(k == 2)
        def _():
            own_column(4)

        @pl.when(jnp.logical_and(k >= 2, k <= 4))
        def _():
            other_column(k - 1, 1 - k)

        @pl.when(k == 5)
        def _():
            other_column(4)

        away = jnp.where(k >= 4, k - 3, k)
        beside = jnp.logical_or(k == 0, k == 7)
        x_a = jnp.where(jnp.logical_and(k >= 4, k <= 6), 1 - x, x)
        x_b = jnp.where(beside, 1 - x, x_a)
        z_b = jnp.where(beside, z + away, z - away)
        chips = (slot(z + away, x_a, 0), slot(z_b, x_b, 0))
        for chip in chips:
            arrived(chip + 1 - core)

        side_rows = [aux[chip + c] for chip in chips for c in (0, 1)]
        wide = replicate(
            [(row[:, b * 128 : b * 128 + 128], OWN) for b in range(3) for row in side_rows]
        )
        t_scale[...] = wide[0:256]
        t_pot[...] = wide[512:768] * (INV_TEMP * LOG2E)
        pieces = jnp.concatenate([held[pl.ds(chip, 2)].reshape(128, 256) for chip in chips])
        scaled = pieces[:, 128:256].astype(F32) * (wide[256:512] / wide[0:256])
        high = scaled.astype(BF16)
        right[:, 0:128] = pieces[:, 0:128]
        right[:, 128:256] = high
        right[:, 256:384] = (scaled - high.astype(F32)).astype(BF16)
        right[:, 384:512] = high

        for n in range(8):
            product = lax.dot_general(
                right[...], left[n * 256 : n * 256 + 256, :], NT, preferred_element_type=F32
            )
            tiles = [slice((2 * n + i) * 128, (2 * n + i) * 128 + 128) for i in range(2)]
            s_scale = [scale_row[:, t] for t in tiles]
            high_mark = [peak[:, t] for t in tiles]
            summed = [total[:, t] for t in tiles]
            for g0 in range(0, 32, 4):
                values = [[], []]
                for g in range(g0, g0 + 4):
                    down8 = slice(g * 8, g * 8 + 8)
                    scale, pot = t_scale[down8, :], t_pot[down8, :]
                    for i, t in enumerate(tiles):
                        value = product[down8, i * 128 : i * 128 + 128] * s_scale[i] * scale + pot
                        at = pl.multiple_of(chips[g // 16] * OWN + (g % 16) * 8, 8)
                        logits[pl.ds(at, 8), t] = value
                        values[i].append(value)
                for i in range(2):
                    mark = jnp.maximum(high_mark[i], tree(jnp.maximum, values[i]))
                    added = tree(jnp.add, [jnp.exp2(value - mark) for value in values[i]])
                    summed[i] = summed[i] * jnp.exp2(high_mark[i] - mark) + added
                    high_mark[i] = mark
            for i, t in enumerate(tiles):
                peak[:, t] = high_mark[i]
                total[:, t] = summed[i]
        return 0

    lax.fori_loop(0, ZS, chunk, 0)

    for k in range(16):
        t = slice(k * 128, k * 128 + 128)
        mark = jnp.max(peak[:, t], axis=0, keepdims=True)
        row_sum = jnp.sum(total[:, t] * jnp.exp2(peak[:, t] - mark), axis=0, keepdims=True)
        row_lse[tgt, k : k + 1, :] = mark + jnp.log2(row_sum)

    def row_copy(group, to):
        return pltpu.make_async_remote_copy(
            src_ref=row_lse.at[group],
            dst_ref=row_lse.at[group],
            send_sem=send.at[2],
            recv_sem=row_recv.at[group],
            device_id={"tgt": to},
            device_id_type=MESH,
        )

    others = [(a, b) for a in (0, 1) for b in range(ZS) if a or b]
    for a, b in sorted(others, key=lambda ab: -2 * ab[0] - min(ab[1], ZS - ab[1])):
        row_copy(tgt, ((tgt // ZS) ^ a) * ZS + ((tgt + b) & (ZS - 1))).start()

    def row_wait(k, _):
        row_copy((tgt + k) & (TGT - 1), tgt).wait_recv()
        return 0

    lax.fori_loop(1, TGT, row_wait, 0)

    every = [row_lse[g] for g in range(TGT)]
    mark = tree(jnp.maximum, every)
    joined = mark + jnp.log2(tree(jnp.add, [jnp.exp2(one - mark) for one in every]))
    mass = smass_ref[...]
    u_ref[...] = TEMP * (mass - LN2 * joined)
    shift = LOG2E * mass - joined
    for k in range(16):
        shift_row[:, k * 128 : k * 128 + 128] = jnp.broadcast_to(shift[k : k + 1, :], (8, 128))

    def col_copy(to):
        return pltpu.make_async_remote_copy(
            src_ref=col_mine.at[pl.ds(to // 2, 1)],
            dst_ref=col_lse.at[pl.ds(src, 1)],
            send_sem=send.at[3],
            recv_sem=col_recv.at[src],
            device_id={"src": to},
            device_id_type=MESH,
        )

    def half(h, _):
        def place(n):
            return (z + 2 + h * 4 + n) & (ZS - 1)

        def lanes(b, _):
            for g in range(32):
                down8 = pl.ds(pl.multiple_of(place(b) * 256 + g * 8, 8), 8)
                values = [
                    logits[down8, k * 128 : k * 128 + 128] + shift_row[:, k * 128 : k * 128 + 128]
                    for k in range(16)
                ]
                mark = tree(jnp.maximum, values)
                at = pl.ds(pl.multiple_of(b * 256 + g * 8, 8), 8)
                lane_peak[at, :] = mark
                lane_sum[at, :] = tree(jnp.add, [jnp.exp2(value - mark) for value in values])
            return 0

        lax.fori_loop(0, 4, lanes, 0)
        for q in range(8):
            at = slice(q * 128, q * 128 + 128)
            peaks, sums = lane_peak[at, :].T, lane_sum[at, :].T
            mark = jnp.max(peaks, axis=0, keepdims=True)
            col_mine[pl.ds(place(q // 2) * 2 + q % 2, 1), :] = mark + jnp.log2(
                jnp.sum(sums * jnp.exp2(peaks - mark), axis=0, keepdims=True)
            )

        def col_push(k, _):
            to = place(k // 4) * 4 + ((src + k) & 3)

            @pl.when(to != src)
            def _():
                col_copy(to).start()

            return 0

        lax.fori_loop(0, 16, col_push, 0)
        return 0

    lax.fori_loop(0, 2, half, 0)
    col_lse[pl.ds(src, 1), :] = col_mine[pl.ds(src // 2, 1), :]

    def col_wait(k, _):
        other = (src + k) & (SRC - 1)
        pltpu.make_async_remote_copy(
            src_ref=col_mine.at[pl.ds(0, 1)],
            dst_ref=col_lse.at[pl.ds(other, 1)],
            send_sem=send.at[3],
            recv_sem=col_recv.at[other],
            device_id={"src": src},
            device_id_type=MESH,
        ).wait_recv()
        return 0

    lax.fori_loop(1, SRC, col_wait, 0)
    partial = col_lse[...]
    mark = jnp.max(partial, axis=0, keepdims=True)
    joined = mark + jnp.log2(jnp.sum(jnp.exp2(partial - mark), axis=0, keepdims=True))
    mine = jnp.where(core == 1, joined[:, 64:128], joined[:, 0:64])
    v_ref[...] = TEMP * (tmass_ref[...] - (LN2 * mine - INV_TEMP * own_pot))

    for k, (buffer, many) in enumerate(
        ((held, SRC - 1), (aux, SRC - 1), (row_lse, TGT - 1), (col_lse, SRC - 1))
    ):
        part = buffer.at[pl.ds(0, many)]
        pltpu.make_async_copy(part, part, send.at[k]).wait()


def per_device(src_codes, src_scales, log_source_mass, tgt_codes, tgt_scales, tgt_potential, log_target_mass):
    vmem = pl.BlockSpec(memory_space=pltpu.VMEM)
    u, v = pl.pallas_call(
        kernel,
        out_shape=(
            jax.ShapeDtypeStruct((16, 128), F32),
            jax.ShapeDtypeStruct((1, OWN), F32),
        ),
        in_specs=[pl.BlockSpec(memory_space=pltpu.HBM)] * 7,
        out_specs=(vmem, vmem),
        scratch_shapes=[
            pltpu.VMEM((ROWS, 256), BF16),
            pltpu.VMEM((2, ROWS), BF16),
            pltpu.VMEM((16, 128), F32),
            pltpu.VMEM((2, OWN), BF16),
            pltpu.VMEM((1, OWN), BF16),
            pltpu.VMEM((1, OWN), F32),
            pltpu.VMEM((SRC, OWN, 256), BF16),
            pltpu.VMEM((SRC, 1, 384), F32),
            pltpu.VMEM((ROWS, 512), BF16),
            pltpu.VMEM((256, 512), BF16),
            pltpu.VMEM((ROWS, ROWS), F32),
            pltpu.VMEM((8, ROWS), F32),
            pltpu.VMEM((8, ROWS), F32),
            pltpu.VMEM((8, ROWS), F32),
            pltpu.VMEM((8, ROWS), F32),
            pltpu.VMEM((256, 128), F32),
            pltpu.VMEM((256, 128), F32),
            pltpu.VMEM((1024, 128), F32),
            pltpu.VMEM((1024, 128), F32),
            pltpu.VMEM((TGT, 16, 128), F32),
            pltpu.VMEM((16, 128), F32),
            pltpu.VMEM((SRC, 128), F32),
            pltpu.SemaphoreType.DMA((SRC,)),
            pltpu.SemaphoreType.DMA((SRC,)),
            pltpu.SemaphoreType.DMA((TGT,)),
            pltpu.SemaphoreType.DMA((SRC,)),
            pltpu.SemaphoreType.DMA((4,)),
            pltpu.SemaphoreType.DMA((7,)),
        ],
        compiler_params=pltpu.CompilerParams(
            collective_id=0, has_side_effects=True, vmem_limit_bytes=62 << 20
        ),
        cost_estimate=pl.CostEstimate(
            flops=2 * ROWS * ROWS * 512, bytes_accessed=2 << 20, transcendentals=2 * ROWS * ROWS
        ),
    )(
        src_codes,
        src_scales.T,
        log_source_mass.reshape(16, 128),
        tgt_codes,
        tgt_scales.T,
        tgt_potential.reshape(1, OWN),
        log_target_mass.reshape(1, OWN),
    )
    return u.reshape(ROWS), v.reshape(OWN)


def solution(mesh):
    return jax.shard_map(
        per_device,
        mesh=mesh,
        in_specs=(
            P("src", None),
            P("src", None),
            P("src"),
            P(("tgt", "src"), None),
            P(("tgt", "src"), None),
            P(("tgt", "src")),
            P(("tgt", "src")),
        ),
        out_specs=(P("src"), P(("tgt", "src"))),
        check_vma=False,
    )
```
